256 devices in a mesh: row: 8 (over x, core), col: 32 (over y, z).
Axes of the slice: x: 4, y: 4, z: 8, core: 2. Of those that a mesh axis runs over, the one named last changes fastest.
Arguments:
- features: bfloat16 [65536, 256], P(('row', 'col')), may hold values from -6 to 6
- neighbours: int32 [10, 65536], P(None, ('row', 'col')), may hold values from 0 to 511, as said below
- halo_ids: int32 [256, 1, 256], P(('row', 'col')), may hold values from 0 to 255
- w_self: bfloat16 [256, 256], replicated, may hold values from -0.375 to 0.375
- w_neigh: bfloat16 [256, 256], replicated, may hold values from -0.75 to 0.75
- b_sage: float32 [256], replicated, may hold values from -3 to 3
- w_first: bfloat16 [512, 256], replicated, may hold values from -0.25 to 0.25
- b_first: float32 [256], replicated, may hold values from -3 to 3
- w_second: bfloat16 [256], replicated, may hold values from -1.5 to 1.5
- b_second: float32 [1], replicated, may hold values from -3 to 3
- src_owner: int32 [8, 32, 8192, 1], P('row', 'col'), may hold values from 0 to 31; in each aligned block of 8192 rows (0 to 8191, 8192 to 16383, ..., all dimensions but the last counted through in order) at most 320 rows name the same one
- src_local: int32 [8, 32, 8192], P('row', 'col'), may hold values from 0 to 255
- dst_index: int32 [8, 32, 8192], P('row', 'col'), may hold values from 0 to 2047
- labels: int32 [8, 32, 8192], P('row', 'col'), may hold values 0 or 1
Outputs:
- embeds: bfloat16 [65536, 256], P(('row', 'col'))
- logits: float32 [8, 32, 8192], P('row', 'col')
- node_grad: float32 [65536, 256], P(('row', 'col'))
- grad_self: float32 [256, 256], replicated
- grad_neigh: float32 [256, 256], replicated
- grad_bsage: float32 [256], replicated
- grad_first: float32 [32, 512, 256], P('col')
- grad_bfirst: float32 [32, 256], P('col')
- grad_second: float32 [32, 256], P('col')
The draws below stay inside these ranges and needn't reach their ends.
Inputs may be any that keep to these rules, and one draw needn't show every extreme that they name: `neighbours`: in each partition every one of the 256 received rows (values 256 and up) is named by exactly one entry; the other entries name the partition's own rows. `src_owner`: among the 8192 edges of one tile at most 320 name the same source partition, and that many are reached.
All inputs are finite; a program needn't handle non-finite values. No bound on the sum of `labels` on one device may be relied on, other than what follows from the above.
Results may differ from the reference program's by a relative error of at most 0.0052.
Values may be sent and summed in bfloat16 or wider, within the bound.
No kernel may reach another device: no remote copies, remote signals or barrier semaphores. Data moves between devices by JAX's collectives and lax.ppermute only.
A program may use at most 128 MiB of HBM per device.

```python
import math
import jax
import jax.numpy as jnp
import numpy as np
from jax import lax

D = 256
HID = 256
FANOUT = 10
HALO = 1
NODE_DEV = 256
E_DEV = 8192
PARTITIONS = 256
NODES = 65536
CAP = 320
N_ROW = 8
N_COL = 32


def draw_neighbours(key, part):
    keys = jax.random.split(jax.random.fold_in(key, 17), PARTITIONS)

    def one_part(part_key):
        first_key, second_key = jax.random.split(part_key)
        order = jax.random.permutation(first_key, FANOUT * NODE_DEV).astype(jnp.int32)
        own_rows = jax.random.randint(second_key, (FANOUT * NODE_DEV,), 0, NODE_DEV, dtype=jnp.int32)
        values = jnp.where(order < HALO * PARTITIONS, NODE_DEV + order, own_rows)
        return values.reshape(FANOUT, NODE_DEV)
    stacked = jax.vmap(one_part)(keys)
    return jnp.transpose(stacked, (1, 0, 2)).reshape(FANOUT, PARTITIONS * NODE_DEV)


def with_ends(drawn, rng, smallest, largest):
    longest = drawn.shape.index(max(drawn.shape))
    spots = []
    for shift in (0, 1):
        where = [jax.random.randint(jax.random.fold_in(rng, axis), (), 0, length) for axis, length in enumerate(drawn.shape)]
        where[longest] = (where[longest] + shift) % drawn.shape[longest]
        spots.append(tuple(where))
    return drawn.at[spots[0]].set(smallest).at[spots[1]].set(largest)


def block_scale(stream_key, dims, shards, low, high):
    def one(dim, parts):
        draws = jax.random.uniform(jax.random.fold_in(jax.random.fold_in(stream_key, 6), dim), (parts,), jnp.float32, low / len(shards), high / len(shards))
        return jnp.repeat(jnp.exp(draws), dims[dim] // parts).reshape((-1,) + (1,) * (len(dims) - dim - 1))

    gain = one(*shards[0])
    for cut in shards[1:]:
        gain = gain * one(*cut)
    return gain


def shared_out(rng, own, number, rows, count, top, limit, slope):
    order = jax.random.permutation(rng, count)
    crowded, usual = portions_of(count, rows * top, limit, slope, True), portions_of(count, rows * top, limit, slope, False)
    places = jnp.arange(count)

    def named(tallies, turn):
        used = int((tallies > 0).sum())
        fixed = max(1, used // 4)
        shifted = fixed + (places - fixed + turn * (used - fixed)) % max(1, count - fixed)
        return jnp.zeros((count,), jnp.int32).at[order[jnp.where(places < fixed, places, shifted)]].set(jnp.asarray(tallies, jnp.int32))

    tallies = jnp.where(number % 4 == 0, named(crowded, number // 4), named(usual, number - number // 4 - 1))
    mixed = jax.random.permutation(jax.random.fold_in(own, 3), count)
    giver, receiver = mixed[0:count // 2 * 2:2], mixed[1:count // 2 * 2:2]
    room = jnp.minimum(tallies[giver] - 1, limit - tallies[receiver]) // 2
    room = jnp.where((giver == order[0]) | (receiver == order[0]) | (tallies[receiver] == 0), 0, jnp.maximum(room, 0))
    shifted = jax.random.randint(jax.random.fold_in(own, 4), (count // 2,), 0, 1 << 20) % (room + 1)
    tallies = tallies.at[giver].add(-shifted).at[receiver].add(shifted)
    members = jnp.searchsorted(jnp.cumsum(tallies), jnp.arange(rows * top), side="right").astype(jnp.int32)
    listing = members.reshape(top, rows).T
    listing = listing[jax.random.permutation(jax.random.fold_in(own, 1), rows)]
    turn = jax.random.randint(jax.random.fold_in(own, 2), (rows, 1), 0, top)
    return jnp.take_along_axis(listing, (jnp.arange(top)[None, :] + turn) % top, axis=1)


def portions_of(count, total, limit, skew, full):
    portions = [(1 << 20) // math.isqrt(grade ** skew) + 1 for grade in range(1, count + 1)]
    largest = limit if full else min(limit, max(-(-total // count), total * portions[0] // sum(portions)))
    least = 1 if total - largest >= count - 1 else 0
    given, spare = [largest] + [least] * (count - 1), total - largest - least * (count - 1)
    while spare > 0:
        movable = [i for i in range(1, count) if given[i] < largest] or [i for i in range(1, count) if given[i] < limit]
        mass, remaining = sum([portions[i] for i in movable]), spare
        for i in movable:
            more = min(limit - given[i], max(1, remaining * portions[i] // mass), spare)
            given[i] = given[i] + more
            spare = spare - more
    return np.array(given)


def normal_values(own_key, shape, scale, limit, pieces=(), kind=jnp.bfloat16):
    entries = scale * jax.random.normal(own_key, shape, jnp.float32)
    if pieces:
        entries = entries * block_scale(own_key, shape, pieces, -0.22, 0.18)
    return jnp.clip(entries, -limit, limit).astype(kind)


def setup_inputs(seed: int = 0) -> dict:
    key_list = jax.random.split(jax.random.key(seed), 15)
    features = normal_values(key_list[0], (NODES, D), 1.0, 6.0, ((0, 256),))
    neighbours = draw_neighbours(jax.random.fold_in(key_list[14], 71), 0)
    halo_ids = with_ends(jax.random.randint(key_list[2], (PARTITIONS, HALO, PARTITIONS), 0, NODE_DEV), jax.random.fold_in(key_list[2], 1), 0, NODE_DEV - 1).astype(jnp.int32)
    w_self = normal_values(key_list[3], (D, D), D ** -0.5, 0.375)
    w_neigh = normal_values(key_list[4], (D, D), (D // 4) ** -0.5, 0.75)
    b_sage = normal_values(key_list[5], (D,), 0.5, 3.0, (), jnp.float32)
    w_first = normal_values(key_list[6], (2 * D, HID), (2 * D) ** -0.5, 0.25)
    b_first = normal_values(key_list[7], (HID,), 0.5, 3.0, (), jnp.float32)
    w_second = normal_values(key_list[8], (HID,), 0.25, 1.5)
    b_second = normal_values(key_list[9], (1,), 1.0, 3.0, (), jnp.float32)
    src_owner_keys = jax.random.split(jax.random.fold_in(key_list[10], 1), N_ROW * N_COL * E_DEV // E_DEV)
    src_owner_turns = jax.random.permutation(jax.random.fold_in(key_list[10], 3), N_ROW * N_COL * E_DEV // E_DEV)
    src_owner = jax.vmap(lambda own, number: shared_out(jax.random.fold_in(key_list[10], 2), own, number, E_DEV, N_COL, 1, CAP, 2))(src_owner_keys, src_owner_turns).reshape((N_ROW, N_COL, E_DEV, 1))
    src_local = with_ends(jax.random.randint(key_list[11], (N_ROW, N_COL, E_DEV), 0, NODE_DEV), jax.random.fold_in(key_list[11], 1), 0, NODE_DEV - 1).astype(jnp.int32)
    dst_index = with_ends(jax.random.randint(key_list[12], (N_ROW, N_COL, E_DEV), 0, N_ROW * NODE_DEV), jax.random.fold_in(key_list[12], 1), 0, (N_ROW * NODE_DEV) - 1).astype(jnp.int32)
    labels = with_ends((jax.random.randint(key_list[13], (N_ROW, N_COL, E_DEV), 0, 2) < 1).astype(jnp.int32), jax.random.fold_in(key_list[13], 1), 0, 1)
    return dict(features=features, neighbours=neighbours, halo_ids=halo_ids, w_self=w_self, w_neigh=w_neigh, b_sage=b_sage, w_first=w_first, b_first=b_first, w_second=w_second, b_second=b_second, src_owner=src_owner, src_local=src_local, dst_index=dst_index, labels=labels)


def encode_one(part_index, features_all, neighbours, halo_ids, w_self, w_neigh, b_sage):
    chosen = halo_ids[:, :, part_index]
    sources = jnp.arange(PARTITIONS, dtype=jnp.int32)[:, None]
    received = features_all[sources, chosen]
    received = jnp.transpose(received, (1, 0, 2)).reshape(HALO * PARTITIONS, D)
    own_rows = features_all[part_index]
    extended = jnp.concatenate([own_rows, received], axis=0)
    picks = lax.dynamic_slice_in_dim(neighbours, (part_index * NODE_DEV).astype(jnp.int32), NODE_DEV, 1)
    gathered = extended[picks].astype(jnp.float32)
    aggregate = (jnp.sum(gathered, axis=0) / FANOUT).astype(jnp.bfloat16)
    embed_f = jnp.dot(own_rows, w_self, preferred_element_type=jnp.float32)
    embed_f = embed_f + jnp.dot(aggregate, w_neigh, preferred_element_type=jnp.float32) + b_sage
    return embed_f.astype(jnp.bfloat16), aggregate


def reference(features, neighbours, halo_ids, w_self, w_neigh, b_sage, w_first, b_first, w_second, b_second, src_owner, src_local, dst_index, labels):
    features_all = features.reshape(PARTITIONS, NODE_DEV, D)
    embeds, aggregate = lax.map(
        lambda part_index: encode_one(part_index, features_all, neighbours, halo_ids, w_self, w_neigh, b_sage),
        jnp.arange(PARTITIONS, dtype=jnp.int32))
    embeds = embeds.reshape(NODES, D)
    aggregate = aggregate.reshape(NODES, D)
    w_src = w_first[:D]
    w_dst = w_first[D:]
    second_f = w_second.astype(jnp.float32)
    owners_all = src_owner.reshape(PARTITIONS, E_DEV)
    locals_all = src_local.reshape(PARTITIONS, E_DEV)
    dests_all = dst_index.reshape(PARTITIONS, E_DEV)
    labels_all = labels.reshape(PARTITIONS, E_DEV)

    def tile_step(sums, inputs):
        node_acc, acc_first, acc_bfirst, acc_second = sums
        tile, owners, local_rows, dest_rows, targets = inputs
        row_of = tile // N_COL
        col_of = tile % N_COL
        src_nodes = (row_of * N_COL + owners) * NODE_DEV + local_rows
        dst_nodes = ((dest_rows // NODE_DEV) * N_COL + col_of) * NODE_DEV + dest_rows % NODE_DEV
        src_embed = embeds[src_nodes]
        dst_embed = embeds[dst_nodes]
        preact = jnp.dot(src_embed, w_src, preferred_element_type=jnp.float32)
        preact = preact + jnp.dot(dst_embed, w_dst, preferred_element_type=jnp.float32) + b_first
        gate_sig = jax.nn.sigmoid(preact)
        hidden = preact * gate_sig
        hidden_b = hidden.astype(jnp.bfloat16)
        tile_logits = jnp.dot(hidden_b, w_second, preferred_element_type=jnp.float32) + b_second[0]
        dlogit = jax.nn.sigmoid(tile_logits) - targets.astype(jnp.float32)
        dpreact = dlogit[:, None] * second_f[None, :] * gate_sig * (1.0 + preact * (1.0 - gate_sig))
        dpreact_b = dpreact.astype(jnp.bfloat16)
        acc_second = acc_second.at[col_of].add(jnp.sum(hidden * dlogit[:, None], axis=0))
        acc_bfirst = acc_bfirst.at[col_of].add(jnp.sum(dpreact, axis=0))
        grad_src = jnp.dot(src_embed.T, dpreact_b, preferred_element_type=jnp.float32)
        grad_dst = jnp.dot(dst_embed.T, dpreact_b, preferred_element_type=jnp.float32)
        acc_first = acc_first.at[col_of].add(jnp.concatenate([grad_src, grad_dst], axis=0))
        src_rows_g = jnp.dot(dpreact_b, w_src.T, preferred_element_type=jnp.float32).astype(jnp.bfloat16)
        dst_rows_g = jnp.dot(dpreact_b, w_dst.T, preferred_element_type=jnp.float32).astype(jnp.bfloat16)
        node_acc = node_acc.at[src_nodes].add(src_rows_g.astype(jnp.float32))
        node_acc = node_acc.at[dst_nodes].add(dst_rows_g.astype(jnp.float32))
        return (node_acc, acc_first, acc_bfirst, acc_second), tile_logits

    start = (jnp.zeros((NODES, D), jnp.float32), jnp.zeros((N_COL, 2 * D, HID), jnp.float32),
             jnp.zeros((N_COL, HID), jnp.float32), jnp.zeros((N_COL, HID), jnp.float32))
    tiles = jnp.arange(PARTITIONS, dtype=jnp.int32)
    sums, logits = lax.scan(tile_step, start, (tiles, owners_all, locals_all, dests_all, labels_all))
    node_grad, grad_first, grad_bfirst, grad_second = sums
    node_grad_b = node_grad.astype(jnp.bfloat16)
    grad_self = jnp.dot(features.T, node_grad_b, preferred_element_type=jnp.float32)
    grad_neigh = jnp.dot(aggregate.T, node_grad_b, preferred_element_type=jnp.float32)
    grad_bsage = jnp.sum(node_grad, axis=0)
    logits = logits.reshape(N_ROW, N_COL, E_DEV)
    return (embeds, logits, node_grad, grad_self, grad_neigh, grad_bsage, grad_first, grad_bfirst, grad_second)
```

```python
import jax
import jax.numpy as jnp
from jax import lax
from jax.experimental import pallas as pl
from jax.experimental.pallas import tpu as pltpu
from jax.sharding import Mesh, PartitionSpec as P

ROW = ("x", "core")
COL = ("y", "z")
ALL = ROW + COL
BLOCK = 512
F32 = jnp.float32
BF16 = jnp.bfloat16


def dot(a, b):
    return jnp.dot(a, b, preferred_element_type=F32)


def dot_tn(a, b):
    return lax.dot_general(a, b, (((0,), (0,)), ((), ())), preferred_element_type=F32)


def one_hot(index, shape, dim):
    spots = lax.broadcasted_iota(jnp.int32, shape, dim).astype(F32)
    return jnp.where(index == spots, 1.0, 0.0).astype(BF16)


def pick(index, value, shape):
    return jnp.broadcast_to(jnp.where(index == value, 1.0, 0.0), shape).astype(BF16)


def outgoing_kernel(ids_ref, feat_ref, out_ref):
    n = feat_ref.shape[0]
    cols = jnp.transpose(jnp.broadcast_to(ids_ref[...], (8, n)).astype(F32))
    out_ref[...] = dot(one_hot(cols[:, 0:1], (n, n), 1), feat_ref[...]).astype(BF16)


def encoder_kernel(neigh_ref, feat_ref, recv_ref, wself_ref, wneigh_ref, bias_ref, agg_ref, emb_ref):
    fanout, n = neigh_ref.shape
    cols = jnp.transpose(neigh_ref[...].astype(F32))
    spots = lax.broadcasted_iota(jnp.int32, (n, 2 * n), 1).astype(F32)
    count = jnp.zeros((n, 2 * n), F32)
    for k in range(fanout):
        count = count + jnp.where(cols[:, k : k + 1] == spots, 1.0, 0.0)
    count = count.astype(BF16)
    total = dot(count[:, :n], feat_ref[...]) + dot(count[:, n:], recv_ref[...])
    agg = (total / fanout).astype(BF16)
    agg_ref[...] = agg
    emb = dot(feat_ref[...], wself_ref[...]) + dot(agg, wneigh_ref[...]) + bias_ref[...]
    emb_ref[...] = emb.astype(BF16)


def decoder_kernel(
    seg_ref, fields_ref, es_ref, ed_ref, w1_ref, w1t_ref, bfirst_ref, w2_ref, b2_ref,
    logit_ref, sgrad_ref, dgrad_ref, gfirst_ref, vec_ref, sacc, dacc, xs,
):
    i = pl.program_id(0)
    d = es_ref.shape[2]
    parts = ed_ref.shape[0]

    @pl.when(i == 0)
    def _():
        sacc[...] = jnp.zeros_like(sacc)
        dacc[...] = jnp.zeros_like(dacc)
        gfirst_ref[...] = jnp.zeros_like(gfirst_ref)
        vec_ref[...] = jnp.zeros_like(vec_ref)

    rows = fields_ref[0]
    cols = jnp.transpose(rows)
    wide = (BLOCK, d)
    tall = (d, BLOCK)
    first = seg_ref[i, 0]
    last = seg_ref[i, 1]

    src_pick = one_hot(cols[:, 1:2], wide, 1)
    xs[...] = jnp.zeros_like(xs)

    def gather_src(o, carry):
        mask = pick(cols[:, 0:1], o.astype(F32), wide)
        xs[...] += dot(src_pick * mask, es_ref[o])
        return carry

    lax.fori_loop(first, last + 1, gather_src, 0)
    dst_pick = one_hot(cols[:, 3:4], wide, 1)
    xd_f = jnp.zeros(wide, F32)
    for h in range(parts):
        xd_f = xd_f + dot(dst_pick * pick(cols[:, 2:3], float(h), wide), ed_ref[h])
    x_src = xs[...].astype(BF16)
    x_dst = xd_f.astype(BF16)

    preact = dot(x_src, w1_ref[:d]) + dot(x_dst, w1_ref[d:]) + bfirst_ref[...]
    sig = jax.nn.sigmoid(preact)
    hidden = preact * sig
    w2 = w2_ref[...]
    logits = jnp.sum(hidden.astype(BF16).astype(F32) * w2, axis=1, keepdims=True) + b2_ref[0, 0]
    dlogit = jax.nn.sigmoid(logits) - cols[:, 4:5]
    dpre = dlogit * w2 * (sig * (1.0 + preact * (1.0 - sig)))
    dpre_b = dpre.astype(BF16)
    logit_ref[0] = jnp.transpose(jnp.broadcast_to(logits, (BLOCK, 128)))[0:1, :]
    vec_ref[1:2, :] += jnp.sum(dpre, axis=0, keepdims=True)
    vec_ref[2:3, :] += jnp.sum(hidden * dlogit, axis=0, keepdims=True)
    gfirst_ref[:d] += dot_tn(x_src, dpre_b)
    gfirst_ref[d:] += dot_tn(x_dst, dpre_b)
    back = dot(dpre_b, w1t_ref[...]).astype(BF16)
    back_src = back[:, :d]
    back_dst = back[:, d:]
    back_f = back_src.astype(F32) + back_dst.astype(F32)
    vec_ref[0:1, :] += jnp.sum(back_f, axis=0, keepdims=True)

    src_put = one_hot(rows[1:2, :], tall, 0)

    def scatter_src(o, carry):
        mask = pick(rows[0:1, :], o.astype(F32), tall)
        sacc[o] += dot(src_put * mask, back_src)
        return carry

    lax.fori_loop(first, last + 1, scatter_src, 0)
    dst_put = one_hot(rows[3:4, :], tall, 0)
    for h in range(parts):
        dacc[h] += dot(dst_put * pick(rows[2:3, :], float(h), tall), back_dst)

    @pl.when(i == pl.num_programs(0) - 1)
    def _():
        sgrad_ref[...] = sacc[...].astype(BF16)
        dgrad_ref[...] = dacc[...].astype(BF16)


def encoder_grad_kernel(fs_ref, as_ref, sg_ref, fd_ref, ad_ref, dg_ref, out_ref):
    i = pl.program_id(0)
    d = fs_ref.shape[1]

    @pl.when(i == 0)
    def _():
        out_ref[...] = jnp.zeros_like(out_ref)

    out_ref[:d] += dot_tn(fs_ref[...], sg_ref[...]) + dot_tn(fd_ref[...], dg_ref[...])
    out_ref[d:] += dot_tn(as_ref[...], sg_ref[...]) + dot_tn(ad_ref[...], dg_ref[...])


def params(mib=48):
    return pltpu.CompilerParams(vmem_limit_bytes=mib * 1024 * 1024)


def a2a(x, axes):
    return lax.all_to_all(x, axes, split_axis=0, concat_axis=0, tiled=True)


def to_all(x, axes, count):
    return a2a(jnp.broadcast_to(x[None], (count,) + x.shape), axes)


def per_device(
    features, neighbours, halo_ids, w_self, w_neigh, b_sage, w_first, b_first,
    w_second, b_second, src_owner, src_local, dst_index, labels,
):
    n, d = features.shape
    nx, nc, ny, nz = (lax.axis_size(a) for a in ALL)
    nrow, ncol = nx * nc, ny * nz
    edges = src_local.shape[2]
    blocks = edges // BLOCK

    f_col = lax.all_gather(lax.all_gather(features, "z"), "y")
    f_row = to_all(features, ROW, nrow)

    outgoing = pl.pallas_call(
        outgoing_kernel, out_shape=jax.ShapeDtypeStruct((n, d), BF16), compiler_params=params()
    )(halo_ids[0], features)
    received = a2a(outgoing.reshape(nrow, ncol, d), ROW)
    received = lax.all_to_all(received, COL, split_axis=1, concat_axis=1, tiled=True)

    key = ((src_owner[0, 0, :, 0] * n + src_local[0, 0]) << 12) | (dst_index[0, 0] << 1) | labels[0, 0]
    key, order = lax.sort((key, lax.iota(jnp.int32, edges)), num_keys=1)
    key = key.reshape(blocks, BLOCK)
    owner = key >> 20
    dst = key >> 1
    zero = jnp.zeros_like(key)
    fields = jnp.stack(
        [owner, (key >> 12) & 255, (dst >> 8) & 7, dst & 255, key & 1, zero, zero, zero], axis=1
    ).astype(F32)
    seg = jnp.stack([owner[:, 0], owner[:, -1]], axis=1)

    agg, embeds = pl.pallas_call(
        encoder_kernel,
        out_shape=(jax.ShapeDtypeStruct((n, d), BF16), jax.ShapeDtypeStruct((n, d), BF16)),
        compiler_params=params(),
    )(neighbours, features, received.reshape(nrow * ncol, d), w_self, w_neigh, b_sage[None])
    a_row = to_all(agg, ROW, nrow)
    a_col = lax.all_gather(lax.all_gather(agg, "z"), "y")

    def embed(f, a):
        e = dot(f.reshape(-1, d), w_self) + dot(a.reshape(-1, d), w_neigh) + b_sage
        return e.astype(BF16).reshape(-1, n, d)

    e_row = embed(f_row, a_row)
    e_col = embed(f_col, a_col)

    def whole(*shape):
        return pl.BlockSpec(shape, lambda i, s: (0,) * len(shape))

    logits, sgrad, dgrad, gfirst, vec = pl.pallas_call(
        decoder_kernel,
        grid_spec=pltpu.PrefetchScalarGridSpec(
            num_scalar_prefetch=1,
            grid=(blocks,),
            in_specs=[
                pl.BlockSpec((1, 8, BLOCK), lambda i, s: (i, 0, 0)),
                whole(ncol, n, d), whole(nrow, n, d), whole(2 * d, d), whole(d, 2 * d),
                whole(1, d), whole(1, d), pl.BlockSpec(memory_space=pltpu.SMEM),
            ],
            out_specs=[
                pl.BlockSpec((1, 1, BLOCK), lambda i, s: (i, 0, 0)),
                whole(ncol, n, d), whole(nrow, n, d), whole(2 * d, d), whole(8, d),
            ],
            scratch_shapes=[
                pltpu.VMEM((ncol, n, d), F32), pltpu.VMEM((nrow, n, d), F32), pltpu.VMEM((BLOCK, d), F32),
            ],
        ),
        out_shape=(
            jax.ShapeDtypeStruct((blocks, 1, BLOCK), F32),
            jax.ShapeDtypeStruct((ncol, n, d), BF16),
            jax.ShapeDtypeStruct((nrow, n, d), BF16),
            jax.ShapeDtypeStruct((2 * d, d), F32),
            jax.ShapeDtypeStruct((8, d), F32),
        ),
        compiler_params=params(),
    )(seg, fields, e_col, e_row, w_first, w_first.T, b_first[None], w_second.astype(F32)[None], b_second[None])

    logits = lax.sort((order, logits.reshape(edges)), num_keys=1)[1].reshape(1, 1, edges)

    from_y = a2a(sgrad.reshape(ny, nz, n, d), "y")
    part_y = jnp.sum(from_y.astype(F32), axis=0).astype(BF16)
    from_z = a2a(part_y, "z")
    from_row = a2a(dgrad, ROW)
    node_grad = jnp.sum(from_z.astype(F32), axis=0) + jnp.sum(from_row.astype(F32), axis=0)

    steps = 8
    big, small = ncol * n // steps, nrow * n // steps
    genc = pl.pallas_call(
        encoder_grad_kernel,
        grid=(steps,),
        in_specs=[pl.BlockSpec((big, d), lambda i: (i, 0))] * 3 + [pl.BlockSpec((small, d), lambda i: (i, 0))] * 3,
        out_specs=pl.BlockSpec((2 * d, d), lambda i: (0, 0)),
        out_shape=jax.ShapeDtypeStruct((2 * d, d), F32),
        compiler_params=params(),
    )(*(v.reshape(-1, d) for v in (f_col, a_col, sgrad, f_row, a_row, dgrad)))

    cut = 2 * d // nrow
    mixed = jnp.concatenate(
        [genc.reshape(nrow, cut, d), gfirst.reshape(nrow, cut, d), jnp.broadcast_to(vec[None], (nrow, 8, d))], axis=1
    )
    mixed = jnp.sum(a2a(mixed, ROW), axis=0)
    vec = mixed[2 * cut :]
    thin = cut // ncol
    over = jnp.concatenate(
        [mixed[:cut].reshape(ncol, thin, d), jnp.broadcast_to(vec[None, 0:1], (ncol, 1, d))], axis=1
    )
    over = jnp.sum(a2a(over, COL), axis=0)
    grad_bsage = over[thin]
    enc_cut = to_all(over[:thin], COL, ncol).reshape(cut, d)
    final = to_all(jnp.concatenate([enc_cut, mixed[cut : 2 * cut]], axis=0), ROW, nrow)
    enc = final[:, :cut].reshape(2 * d, d)
    dec = final[:, cut:].reshape(2 * d, d)
    return (
        embeds, logits, node_grad, enc[:d], enc[d:], grad_bsage, dec[None], vec[1:2], vec[2:3],
    )


def solution(mesh):
    fine = Mesh(mesh.devices.reshape(mesh.shape["row"] // 2, 2, mesh.shape["col"] // 8, 8), ALL)
    edge = P(ROW, COL, None)
    placed = (
        P(ALL, None), P(None, ALL), P(ALL, None, None),
        P(), P(), P(), P(), P(), P(), P(),
        P(ROW, COL, None, None), edge, edge, edge,
    )
    return jax.shard_map(
        per_device,
        mesh=fine,
        in_specs=placed,
        out_specs=(
            P(ALL, None), edge, P(ALL, None), P(), P(), P(),
            P(COL, None, None), P(COL, None), P(COL, None),
        ),
        check_vma=False,
    )
```

```python
import functools

import jax
import jax.numpy as jnp
from jax import lax
from jax.experimental import pallas as pl
from jax.experimental.pallas import tpu as pltpu
from jax.sharding import Mesh, PartitionSpec as P

ROW = ("x", "core")
COL = ("y", "z")
ALL = ROW + COL
BLOCK = 512
WINDOW = 512
SUB = 64
F32 = jnp.float32
BF16 = jnp.bfloat16


def dot(a, b):
    return jnp.dot(a, b, preferred_element_type=F32)


def dot_tn(a, b):
    return lax.dot_general(a, b, (((0,), (0,)), ((), ())), preferred_element_type=F32)


def one_hot(index, shape, dim):
    spots = lax.broadcasted_iota(jnp.int32, shape, dim).astype(F32)
    return jnp.where(index == spots, 1.0, 0.0).astype(BF16)


def dot_nt(a, b):
    return lax.dot_general(a, b, (((1,), (1,)), ((), ())), preferred_element_type=F32)


def only(picks, owner, value):
    return jnp.where(owner == jnp.asarray(value).astype(BF16), picks, jnp.zeros_like(picks))


def outgoing_kernel(ids_ref, feat_ref, out_ref):
    n = feat_ref.shape[0]
    cols = jnp.transpose(jnp.broadcast_to(ids_ref[...], (8, n)).astype(F32))
    out_ref[...] = dot(one_hot(cols[:, 0:1], (n, n), 1), feat_ref[...]).astype(BF16)


def encoder_kernel(neigh_ref, feat_ref, recv_ref, wself_ref, wneigh_ref, agg_ref, emb_ref):
    fanout, n = neigh_ref.shape
    cols = jnp.transpose(neigh_ref[...].astype(F32))
    spots = lax.broadcasted_iota(jnp.int32, (n, 2 * n), 1).astype(F32)
    count = jnp.zeros((n, 2 * n), F32)
    for k in range(fanout):
        count = count + jnp.where(cols[:, k : k + 1] == spots, 1.0, 0.0)
    count = count.astype(BF16)
    total = dot(count[:, :n], feat_ref[...]) + dot(count[:, n:], recv_ref[...])
    agg = (total / fanout).astype(BF16)
    agg_ref[...] = agg
    emb_ref[...] = dot(feat_ref[...], wself_ref[...]) + dot(agg, wneigh_ref[...])


def decoder_kernel(base, count, closing, *refs):
    start_ref, fields_ref = refs[:2]
    es_refs = refs[2 : 2 + count]
    ed_ref, w1_ref, bfirst_ref, w2_ref, w2r_ref, b2_ref, logit_in, dacc_in, sums_in = refs[2 + count : 11 + count]
    logit_ref, dacc, sums_ref, qs_ref = refs[11 + count : 15 + count]
    qd_ref = refs[15 + count] if closing else None
    xs, dp, pick_d, put_d, pre, hid = refs[-6:]
    ny, n, d = es_refs[0].shape
    dst_parts = ed_ref.shape[0]
    half = 128
    first = start_ref[base]
    last = start_ref[base + ny * count]
    low = float(base * n)
    high = float((base + ny * count) * n)
    origin = pl.multiple_of((first >> 7) << 7, half)
    blocks = (last - origin + BLOCK - 1) // BLOCK
    logit_ref[...] = logit_in[...]
    dacc[...] = dacc_in[...]
    sums_ref[...] = sums_in[...]
    xs[...] = jnp.zeros_like(xs)
    after = pl.multiple_of(origin + blocks * BLOCK, half)
    dp[pl.ds(after, WINDOW)] = jnp.zeros((WINDOW, d), BF16)

    def window(o):
        at = pl.multiple_of((start_ref[o] >> 7) << 7, half)
        return at, fields_ref[:, pl.ds(at, WINDOW)]

    for j in range(count):
        for y in range(ny):
            o = base + j * ny + y
            at, rows = window(o)
            col = jnp.transpose(rows)[:, 0:1] - float(o * n)
            xs[pl.ds(at, WINDOW)] += dot(one_hot(col, (WINDOW, n), 1), es_refs[j][y]).astype(BF16)

    def block(i, carry):
        at = pl.multiple_of(origin + i * BLOCK, half)
        rows = fields_ref[:, pl.ds(at, BLOCK)]
        cols = jnp.transpose(rows)
        wide = (BLOCK, n)
        tall = (n, BLOCK)
        dst_pick = one_hot(cols[:, 2:3], wide, 1)
        dst_owner = jnp.broadcast_to(cols[:, 1:2], wide).astype(BF16)
        for h in range(dst_parts):
            pick_d[:, h * n : (h + 1) * n] = only(dst_pick, dst_owner, float(h))
        x_dst = dot(pick_d[...], ed_ref[...].reshape(dst_parts * n, d)).astype(BF16)
        pre[...] = dot(xs[pl.ds(at, BLOCK)], w1_ref[:d]) + dot(x_dst, w1_ref[d:])
        inside = jnp.where((cols[:, 0:1] >= low) & (cols[:, 0:1] < high), 1.0, 0.0)

        for k in range(0, BLOCK, SUB):
            p = pre[k : k + SUB] + bfirst_ref[...]
            s = 0.5 * jnp.tanh(0.5 * p) + 0.5
            hid[k : k + SUB] = (p * s).astype(BF16)
        score = dot(hid[...], w2r_ref[...]) + b2_ref[0, 0]
        eye = lax.broadcasted_iota(jnp.int32, (half, half), 0) == lax.broadcasted_iota(jnp.int32, (half, half), 1)
        out = [
            jnp.sum(jnp.where(eye, score[k : k + half], 0.0), axis=0, keepdims=True) for k in range(0, BLOCK, half)
        ]
        inside_t = (rows[0:1, :] >= low) & (rows[0:1, :] < high)
        logit_ref[:, pl.ds(at, BLOCK)] = jnp.where(
            inside_t, jnp.concatenate(out, axis=1), logit_ref[:, pl.ds(at, BLOCK)]
        )
        sum_p = jnp.zeros((1, d), F32)
        sum_h = jnp.zeros((1, d), F32)
        for k in range(0, BLOCK, SUB):
            p = pre[k : k + SUB] + bfirst_ref[...]
            s = 0.5 * jnp.tanh(0.5 * p) + 0.5
            h = p * s
            g = (0.5 * jnp.tanh(0.5 * score[k : k + SUB]) + 0.5) - cols[k : k + SUB, 3:4]
            g = g * inside[k : k + SUB]
            g = jnp.concatenate([g, g], axis=1)
            e = g * w2_ref[...] * (s + h * (1.0 - s))
            dp[pl.ds(at + k, SUB)] = e.astype(BF16)
            sum_p = sum_p + jnp.sum(e, axis=0, keepdims=True)
            sum_h = sum_h + jnp.sum(h * g, axis=0, keepdims=True)
        sums_ref[2 * d : 2 * d + 1, :] += sum_p
        sums_ref[2 * d + 1 : 2 * d + 2, :] += sum_h
        dst_put = one_hot(rows[2:3, :], tall, 0)
        dst_owner_t = jnp.broadcast_to(rows[1:2, :], tall).astype(BF16)
        for h in range(dst_parts):
            put_d[h * n : (h + 1) * n, :] = only(dst_put, dst_owner_t, float(h))
        dacc[...] += dot(put_d[...], dp[pl.ds(at, BLOCK)])
        return carry

    lax.fori_loop(0, blocks, block, 0)

    for j in range(count):
        for y in range(ny):
            o = base + j * ny + y
            at, rows = window(o)
            put = one_hot(rows[0:1, :] - float(o * n), (n, WINDOW), 0)
            q = dot(put, dp[pl.ds(at, WINDOW)]).astype(BF16)
            qs_ref[y, j] = q
            sums_ref[:d] += dot_tn(es_refs[j][y], q)

    if closing:
        for h in range(dst_parts):
            q = dacc[h * n : (h + 1) * n].astype(BF16)
            qd_ref[h] = q
            sums_ref[d : 2 * d] += dot_tn(ed_ref[h], q)


def node_kernel(*refs):
    ps_refs = refs[:-7]
    pd_ref, feat_ref, agg_ref, w1_ref, node_ref, genc_ref, vec_ref = refs[-7:]
    d = feat_ref.shape[1]

    def total(ref):
        out = ref[0].astype(F32)
        for k in range(1, ref.shape[0]):
            out = out + ref[k].astype(F32)
        return out

    def times_wt(q, w):
        high = q.astype(BF16)
        low = (q - high.astype(F32)).astype(BF16)
        return dot_nt(high, w) + dot_nt(low, w)

    from_src = ps_refs[0][...].astype(F32)
    for ref in ps_refs[1:]:
        from_src = from_src + ref[...].astype(F32)
    grad = times_wt(from_src, w1_ref[:d]) + times_wt(total(pd_ref), w1_ref[d:])
    node_ref[...] = grad
    grad_b = grad.astype(BF16)
    genc_ref[:d] = dot_tn(feat_ref[...], grad_b)
    genc_ref[d:] = dot_tn(agg_ref[...], grad_b)
    vec_ref[...] = jnp.broadcast_to(jnp.sum(grad, axis=0, keepdims=True), vec_ref.shape)


def params(mib=48):
    return pltpu.CompilerParams(vmem_limit_bytes=mib * 1024 * 1024)


def a2a(x, axes):
    return lax.all_to_all(x, axes, split_axis=0, concat_axis=0, tiled=True)


def to_all(x, axes, count):
    return a2a(jnp.broadcast_to(x[None], (count,) + x.shape), axes)


def decoder(base, closing, start, fields, es, e_row, w_first, b_first, w_second, b_second, logit, dacc, sums):
    ny, n, d = es[0].shape
    nrow = e_row.shape[0]
    count = len(es)
    length = fields.shape[1]
    vmem = pl.BlockSpec(memory_space=pltpu.VMEM)
    smem = pl.BlockSpec(memory_space=pltpu.SMEM)
    outs = [
        jax.ShapeDtypeStruct(logit.shape, F32),
        jax.ShapeDtypeStruct(dacc.shape, F32),
        jax.ShapeDtypeStruct(sums.shape, F32),
        jax.ShapeDtypeStruct((ny, count, n, d), BF16),
    ]
    if closing:
        outs.append(jax.ShapeDtypeStruct((nrow, n, d), BF16))
    share = count * ny * fields.shape[1] // 32
    return pl.pallas_call(
        functools.partial(decoder_kernel, base, count, closing),
        in_specs=[smem] + [vmem] * (6 + count) + [smem] + [vmem] * 3,
        out_specs=[vmem] * len(outs),
        scratch_shapes=[
            pltpu.VMEM((length, d), BF16), pltpu.VMEM((length, d), BF16),
            pltpu.VMEM((BLOCK, nrow * n), BF16), pltpu.VMEM((nrow * n, BLOCK), BF16),
            pltpu.VMEM((BLOCK, d), F32), pltpu.VMEM((BLOCK, d), BF16),
        ],
        out_shape=outs,
        compiler_params=params(),
        cost_estimate=pl.CostEstimate(
            flops=share * d * (4 * nrow * n + 8 * n), bytes_accessed=8 * 1024 * 1024, transcendentals=2 * share * d
        ),
    )(
        start, fields, *es, e_row, w_first, b_first, w_second.astype(F32)[None],
        jnp.broadcast_to(w_second[:, None], (d, 128)), b_second, logit, dacc, sums,
    )


def per_device(
    features, neighbours, halo_ids, w_self, w_neigh, b_sage, w_first, b_first,
    w_second, b_second, src_owner, src_local, dst_index, labels,
):
    n, d = features.shape
    nx, nc, ny, nz = (lax.axis_size(a) for a in ALL)
    nrow, ncol = nx * nc, ny * nz
    edges = src_local.shape[2]

    outgoing = pl.pallas_call(
        outgoing_kernel, out_shape=jax.ShapeDtypeStruct((n, d), BF16), compiler_params=params()
    )(halo_ids[0], features)
    received = a2a(outgoing.reshape(nrow, ncol, d), ROW)
    received = lax.all_to_all(received, COL, split_axis=1, concat_axis=1, tiled=True)

    ahead = ((src_owner[0, 0, :, 0] & (nz - 1)) - lax.axis_index("z")) & (nz - 1)
    rank = jnp.where(ahead == 0, 0, jnp.where(ahead <= nz // 2, 2 * ahead - 1, 2 * (nz - ahead)))
    slot = rank * ny + src_owner[0, 0, :, 0] // nz
    key = ((slot * n + src_local[0, 0]) << 12) | (dst_index[0, 0] << 1) | labels[0, 0]
    key, order = lax.sort((key, lax.iota(jnp.int32, edges)), num_keys=1)
    row = key >> 12
    zero = jnp.zeros_like(key)
    fields = jnp.stack([row, (key >> 9) & 7, (key >> 1) & 255, key & 1, zero, zero, zero, zero]).astype(F32)
    fields = jnp.pad(fields, ((0, 0), (0, WINDOW + BLOCK)), constant_values=-1.0)
    owners = lax.iota(jnp.int32, ncol + 1)
    start = jnp.sum((row[None, :] < (owners * n)[:, None]).astype(jnp.int32), axis=1)

    agg, emb_f = pl.pallas_call(
        encoder_kernel,
        out_shape=(jax.ShapeDtypeStruct((n, d), BF16), jax.ShapeDtypeStruct((n, d), F32)),
        compiler_params=params(),
    )(neighbours, features, received.reshape(nrow * ncol, d), w_self, w_neigh)
    emb_f, fields, start = lax.optimization_barrier((emb_f, fields, start))
    embeds = (emb_f + b_sage).astype(BF16)
    e_y = lax.all_gather(embeds, "y")

    def shift(x, by):
        return lax.ppermute(x, "z", [(i, (i + by) % nz) for i in range(nz)])

    at = {0: e_y}
    up, down = e_y, e_y
    for k in range(1, nz // 2 + 1):
        down = shift(down, -1)
        at[k] = down
        if k < nz // 2:
            up = shift(up, 1)
            at[nz - k] = up
    e_row = jnp.concatenate(
        [lax.all_gather(embeds[:, : d // 2], ROW), lax.all_gather(embeds[:, d // 2 :], ROW)], axis=2
    )

    groups = ((0,), (1, 7), (2, 6), (3, 5, 4))
    logit = jnp.zeros((1, edges + BLOCK), F32)
    dacc = jnp.zeros((nrow * n, d), F32)
    sums = jnp.zeros((2 * d + 8, d), F32)
    parts = []
    base = 0
    for g, group in enumerate(groups):
        out = decoder(
            base, g == len(groups) - 1, start, fields, [at[k] for k in group], e_row, w_first,
            b_first[None], w_second, b_second[None], logit, dacc, sums,
        )
        logit, dacc, sums, qs = out[:4]
        base += len(group) * ny
        part = jnp.sum(a2a(qs, "y").astype(F32), axis=0).astype(BF16)
        for j, k in enumerate(group):
            parts.append(shift(part[j], k) if k else part[j])
    qd = out[4]

    logits = lax.sort((order, logit[0, :edges]), num_keys=1)[1].reshape(1, 1, edges)
    sums = lax.psum(sums, ROW)
    dec, vec = sums[: 2 * d], sums[2 * d :]
    from_row = a2a(qd, ROW)

    node_grad, genc, bsage = pl.pallas_call(
        node_kernel,
        out_shape=(
            jax.ShapeDtypeStruct((n, d), F32),
            jax.ShapeDtypeStruct((2 * d, d), F32),
            jax.ShapeDtypeStruct((8, d), F32),
        ),
        compiler_params=params(),
    )(*parts, from_row, features, agg, w_first)

    cut = 2 * d // nrow
    thin = cut // ncol
    mixed = jnp.concatenate(
        [genc.reshape(nrow, cut, d), jnp.broadcast_to(bsage[None], (nrow, 8, d))], axis=1
    )
    mixed = jnp.sum(a2a(mixed, ROW), axis=0)
    over = jnp.concatenate(
        [mixed[:cut].reshape(ncol, thin, d), jnp.broadcast_to(mixed[None, cut : cut + 1], (ncol, 1, d))], axis=1
    )
    over = jnp.sum(a2a(over, COL), axis=0)
    grad_bsage = over[thin]
    enc = to_all(over[:thin], COL, ncol).reshape(cut, d)
    enc = to_all(enc, ROW, nrow).reshape(2 * d, d)
    return (
        embeds, logits, node_grad, enc[:d], enc[d:], grad_bsage, dec[None], vec[0:1], vec[1:2],
    )


def solution(mesh):
    fine = Mesh(mesh.devices.reshape(mesh.shape["row"] // 2, 2, mesh.shape["col"] // 8, 8), ALL)
    edge = P(ROW, COL, None)
    placed = (
        P(ALL, None), P(None, ALL), P(ALL, None, None),
        P(), P(), P(), P(), P(), P(), P(),
        P(ROW, COL, None, None), edge, edge, edge,
    )
    return jax.shard_map(
        per_device,
        mesh=fine,
        in_specs=placed,
        out_specs=(
            P(ALL, None), edge, P(ALL, None), P(), P(), P(),
            P(COL, None, None), P(COL, None), P(COL, None),
        ),
        check_vma=False,
    )
```

```python
import functools

import jax
import jax.numpy as jnp
from jax import lax
from jax.experimental import pallas as pl
from jax.experimental.pallas import tpu as pltpu
from jax.sharding import Mesh, PartitionSpec as P

ROW = ("x", "core")
COL = ("y", "z")
ALL = ROW + COL
BLOCK = 512
WINDOW = 512
SUB = 64
F32 = jnp.float32
BF16 = jnp.bfloat16


def dot(a, b):
    return jnp.dot(a, b, preferred_element_type=F32)


def dot_tn(a, b):
    return lax.dot_general(a, b, (((0,), (0,)), ((), ())), preferred_element_type=F32)


def one_hot(index, shape, dim):
    spots = lax.broadcasted_iota(jnp.int32, shape, dim).astype(F32)
    return jnp.where(index == spots, 1.0, 0.0).astype(BF16)


def dot_nt(a, b):
    return lax.dot_general(a, b, (((1,), (1,)), ((), ())), preferred_element_type=F32)


def only(picks, owner, value):
    return jnp.where(owner == jnp.asarray(value).astype(BF16), picks, jnp.zeros_like(picks))


def outgoing_kernel(ids_ref, feat_ref, out_ref):
    n = feat_ref.shape[0]
    cols = jnp.transpose(jnp.broadcast_to(ids_ref[...], (8, n)).astype(F32))
    out_ref[...] = dot(one_hot(cols[:, 0:1], (n, n), 1), feat_ref[...]).astype(BF16)


def encoder_kernel(neigh_ref, feat_ref, recv_ref, wself_ref, wneigh_ref, agg_ref, emb_ref):
    fanout, n = neigh_ref.shape
    cols = jnp.transpose(neigh_ref[...].astype(F32))
    spots = lax.broadcasted_iota(jnp.int32, (n, 2 * n), 1).astype(F32)
    count = jnp.zeros((n, 2 * n), F32)
    for k in range(fanout):
        count = count + jnp.where(cols[:, k : k + 1] == spots, 1.0, 0.0)
    count = count.astype(BF16)
    total = dot(count[:, :n], feat_ref[...]) + dot(count[:, n:], recv_ref[...])
    agg = (total / fanout).astype(BF16)
    agg_ref[...] = agg
    emb_ref[...] = dot(feat_ref[...], wself_ref[...]) + dot(agg, wneigh_ref[...])


def decoder_kernel(base, count, closing, *refs):
    start_ref, fields_ref = refs[:2]
    es_refs = refs[2 : 2 + count]
    ed_ref, w1_ref, bfirst_ref, w2_ref, w2r_ref, b2_ref = refs[2 + count : 8 + count]
    at_out = 8 + count if base == 0 else 11 + count
    so_far = refs[8 + count : at_out]
    logit_ref, dacc, sums_ref, qs_ref = refs[at_out : at_out + 4]
    qd_ref = refs[at_out + 4] if closing else None
    xs, dp, pick_d, put_d, pre, hid = refs[-6:]
    ny, n, d = es_refs[0].shape
    dst_parts = ed_ref.shape[0]
    half = 128
    first = start_ref[base]
    last = start_ref[base + ny * count]
    low = float(base * n)
    high = float((base + ny * count) * n)
    origin = pl.multiple_of((first >> 7) << 7, half)
    blocks = (last - origin + BLOCK - 1) // BLOCK
    for k, ref in enumerate((logit_ref, dacc, sums_ref)):
        ref[...] = so_far[k][...] if so_far else jnp.zeros_like(ref)
    xs[...] = jnp.zeros_like(xs)
    after = pl.multiple_of(origin + blocks * BLOCK, half)
    dp[pl.ds(after, WINDOW)] = jnp.zeros((WINDOW, d), BF16)

    def window(o):
        at = pl.multiple_of((start_ref[o] >> 7) << 7, half)
        return at, fields_ref[:, pl.ds(at, WINDOW)]

    for j in range(count):
        for y in range(ny):
            o = base + j * ny + y
            at, rows = window(o)
            col = jnp.transpose(rows)[:, 0:1] - float(o * n)
            xs[pl.ds(at, WINDOW)] += dot(one_hot(col, (WINDOW, n), 1), es_refs[j][y]).astype(BF16)

    def block(i, carry):
        at = pl.multiple_of(origin + i * BLOCK, half)
        rows = fields_ref[:, pl.ds(at, BLOCK)]
        cols = jnp.transpose(rows)
        wide = (BLOCK, n)
        tall = (n, BLOCK)
        dst_pick = one_hot(cols[:, 2:3], wide, 1)
        dst_owner = jnp.broadcast_to(cols[:, 1:2], wide).astype(BF16)
        for h in range(dst_parts):
            pick_d[:, h * n : (h + 1) * n] = only(dst_pick, dst_owner, float(h))
        x_dst = dot(pick_d[...], ed_ref[...].reshape(dst_parts * n, d)).astype(BF16)
        pre[...] = dot(xs[pl.ds(at, BLOCK)], w1_ref[:d]) + dot(x_dst, w1_ref[d:])
        inside = jnp.where((cols[:, 0:1] >= low) & (cols[:, 0:1] < high), 1.0, 0.0)

        for k in range(0, BLOCK, SUB):
            p = pre[k : k + SUB] + bfirst_ref[...]
            s = 0.5 * jnp.tanh(0.5 * p) + 0.5
            hid[k : k + SUB] = (p * s).astype(BF16)
        score = dot(hid[...], w2r_ref[...]) + b2_ref[0, 0]
        eye = lax.broadcasted_iota(jnp.int32, (half, half), 0) == lax.broadcasted_iota(jnp.int32, (half, half), 1)
        out = [
            jnp.sum(jnp.where(eye, score[k : k + half], 0.0), axis=0, keepdims=True) for k in range(0, BLOCK, half)
        ]
        inside_t = (rows[0:1, :] >= low) & (rows[0:1, :] < high)
        logit_ref[:, pl.ds(at, BLOCK)] = jnp.where(
            inside_t, jnp.concatenate(out, axis=1), logit_ref[:, pl.ds(at, BLOCK)]
        )
        sum_p = jnp.zeros((1, d), F32)
        sum_h = jnp.zeros((1, d), F32)
        for k in range(0, BLOCK, SUB):
            p = pre[k : k + SUB] + bfirst_ref[...]
            s = 0.5 * jnp.tanh(0.5 * p) + 0.5
            h = p * s
            g = (0.5 * jnp.tanh(0.5 * score[k : k + SUB]) + 0.5) - cols[k : k + SUB, 3:4]
            g = g * inside[k : k + SUB]
            g = jnp.concatenate([g, g], axis=1)
            e = g * w2_ref[...] * (s + h * (1.0 - s))
            dp[pl.ds(at + k, SUB)] = e.astype(BF16)
            sum_p = sum_p + jnp.sum(e, axis=0, keepdims=True)
            sum_h = sum_h + jnp.sum(h * g, axis=0, keepdims=True)
        sums_ref[2 * d : 2 * d + 1, :] += sum_p
        sums_ref[2 * d + 1 : 2 * d + 2, :] += sum_h
        dst_put = one_hot(rows[2:3, :], tall, 0)
        dst_owner_t = jnp.broadcast_to(rows[1:2, :], tall).astype(BF16)
        for h in range(dst_parts):
            put_d[h * n : (h + 1) * n, :] = only(dst_put, dst_owner_t, float(h))
        dacc[...] += dot(put_d[...], dp[pl.ds(at, BLOCK)])
        return carry

    lax.fori_loop(0, blocks, block, 0)

    for j in range(count):
        for y in range(ny):
            o = base + j * ny + y
            at, rows = window(o)
            put = one_hot(rows[0:1, :] - float(o * n), (n, WINDOW), 0)
            q = dot(put, dp[pl.ds(at, WINDOW)]).astype(BF16)
            qs_ref[y, j] = q
            sums_ref[:d] += dot_tn(es_refs[j][y], q)

    if closing:
        for h in range(dst_parts):
            q = dacc[h * n : (h + 1) * n].astype(BF16)
            qd_ref[h] = q
            sums_ref[d : 2 * d] += dot_tn(ed_ref[h], q)


def node_kernel(*refs):
    ps_refs = refs[:-7]
    pd_ref, feat_ref, agg_ref, w1_ref, node_ref, genc_ref, vec_ref = refs[-7:]
    d = feat_ref.shape[1]

    def total(ref):
        out = ref[0].astype(F32)
        for k in range(1, ref.shape[0]):
            out = out + ref[k].astype(F32)
        return out

    def times_wt(q, w):
        high = q.astype(BF16)
        low = (q - high.astype(F32)).astype(BF16)
        return dot_nt(high, w) + dot_nt(low, w)

    from_src = ps_refs[0][...].astype(F32)
    for ref in ps_refs[1:]:
        from_src = from_src + ref[...].astype(F32)
    grad = times_wt(from_src, w1_ref[:d]) + times_wt(total(pd_ref), w1_ref[d:])
    node_ref[...] = grad
    grad_b = grad.astype(BF16)
    genc_ref[:d] = dot_tn(feat_ref[...], grad_b)
    genc_ref[d:] = dot_tn(agg_ref[...], grad_b)
    vec_ref[...] = jnp.broadcast_to(jnp.sum(grad, axis=0, keepdims=True), vec_ref.shape)


def params(mib=48):
    return pltpu.CompilerParams(vmem_limit_bytes=mib * 1024 * 1024)


def a2a(x, axes):
    return lax.all_to_all(x, axes, split_axis=0, concat_axis=0, tiled=True)


def to_all(x, axes, count):
    return a2a(jnp.broadcast_to(x[None], (count,) + x.shape), axes)


def decoder(base, closing, start, fields, es, e_row, w_first, b_first, w_second, b_second, *so_far):
    ny, n, d = es[0].shape
    nrow = e_row.shape[0]
    count = len(es)
    length = fields.shape[1]
    vmem = pl.BlockSpec(memory_space=pltpu.VMEM)
    smem = pl.BlockSpec(memory_space=pltpu.SMEM)
    outs = [
        jax.ShapeDtypeStruct((1, length - WINDOW), F32),
        jax.ShapeDtypeStruct((nrow * n, d), F32),
        jax.ShapeDtypeStruct((2 * d + 8, d), F32),
        jax.ShapeDtypeStruct((ny, count, n, d), BF16),
    ]
    if closing:
        outs.append(jax.ShapeDtypeStruct((nrow, n, d), BF16))
    share = count * ny * fields.shape[1] // 32
    return pl.pallas_call(
        functools.partial(decoder_kernel, base, count, closing),
        in_specs=[smem] + [vmem] * (6 + count) + [smem] + [vmem] * len(so_far),
        out_specs=[vmem] * len(outs),
        scratch_shapes=[
            pltpu.VMEM((length, d), BF16), pltpu.VMEM((length, d), BF16),
            pltpu.VMEM((BLOCK, nrow * n), BF16), pltpu.VMEM((nrow * n, BLOCK), BF16),
            pltpu.VMEM((BLOCK, d), F32), pltpu.VMEM((BLOCK, d), BF16),
        ],
        out_shape=outs,
        compiler_params=params(),
        cost_estimate=pl.CostEstimate(
            flops=share * d * (4 * nrow * n + 8 * n), bytes_accessed=8 * 1024 * 1024, transcendentals=2 * share * d
        ),
    )(
        start, fields, *es, e_row, w_first, b_first, w_second.astype(F32)[None],
        jnp.broadcast_to(w_second[:, None], (d, 128)), b_second, *so_far,
    )


def per_device(
    features, neighbours, halo_ids, w_self, w_neigh, b_sage, w_first, b_first,
    w_second, b_second, src_owner, src_local, dst_index, labels,
):
    n, d = features.shape
    nx, nc, ny, nz = (lax.axis_size(a) for a in ALL)
    nrow, ncol = nx * nc, ny * nz
    edges = src_local.shape[2]

    outgoing = pl.pallas_call(
        outgoing_kernel, out_shape=jax.ShapeDtypeStruct((n, d), BF16), compiler_params=params()
    )(halo_ids[0], features)
    received = a2a(outgoing.reshape(nrow, ncol, d), ROW)
    received = lax.all_to_all(received, COL, split_axis=1, concat_axis=1, tiled=True)

    ahead = ((src_owner[0, 0, :, 0] & (nz - 1)) - lax.axis_index("z")) & (nz - 1)
    rank = jnp.where(ahead == 0, 0, jnp.where(ahead <= nz // 2, 2 * ahead - 1, 2 * (nz - ahead)))
    slot = rank * ny + src_owner[0, 0, :, 0] // nz
    key = ((slot * n + src_local[0, 0]) << 12) | (dst_index[0, 0] << 1) | labels[0, 0]
    key, order = lax.sort((key, lax.iota(jnp.int32, edges)), num_keys=1)
    row = key >> 12
    zero = jnp.zeros_like(key)
    fields = jnp.stack([row, (key >> 9) & 7, (key >> 1) & 255, key & 1, zero, zero, zero, zero]).astype(F32)
    fields = jnp.pad(fields, ((0, 0), (0, WINDOW + BLOCK)), constant_values=-1.0)
    owners = lax.iota(jnp.int32, ncol + 1)
    start = jnp.sum((row[None, :] < (owners * n)[:, None]).astype(jnp.int32), axis=1)

    agg, emb_f = pl.pallas_call(
        encoder_kernel,
        out_shape=(jax.ShapeDtypeStruct((n, d), BF16), jax.ShapeDtypeStruct((n, d), F32)),
        compiler_params=params(),
    )(neighbours, features, received.reshape(nrow * ncol, d), w_self, w_neigh)
    emb_f, fields, start = lax.optimization_barrier((emb_f, fields, start))
    embeds = (emb_f + b_sage).astype(BF16)
    e_y = lax.all_gather(embeds, "y")

    def shift(x, by):
        return lax.ppermute(x, "z", [(i, (i + by) % nz) for i in range(nz)])

    at = {0: e_y}
    up, down = e_y, e_y
    for k in range(1, nz // 2 + 1):
        down = shift(down, -1)
        at[k] = down
        if k < nz // 2:
            up = shift(up, 1)
            at[nz - k] = up
    e_row = to_all(embeds, ROW, nrow)

    def send(part, group):
        return [shift(part[j], k) if k else part[j] for j, k in enumerate(group)]

    groups = ((0, 1, 7), (2, 6, 3), (5, 4))
    carry, parts, pending = (), [], []
    base = 0
    for g, group in enumerate(groups):
        closing = g == len(groups) - 1
        if closing:
            carry, pending[0] = lax.optimization_barrier((carry, pending[0]))
            parts += send(pending[0], groups[0])
        out = decoder(
            base, closing, start, fields, [at[k] for k in group], e_row, w_first,
            b_first[None], w_second, b_second[None], *carry,
        )
        carry, qs = out[:3], out[3]
        base += len(group) * ny
        if closing:
            qs, parts = lax.optimization_barrier((qs, parts))
        pending.append(jnp.sum(a2a(qs, "y").astype(F32), axis=0).astype(BF16))
    for k in range(1, len(groups)):
        parts = parts + send(pending[k], groups[k])
    logit, _, sums = carry
    qd = out[4]

    logits = lax.sort((order, logit[0, :edges]), num_keys=1)[1].reshape(1, 1, edges)
    from_row = a2a(qd, ROW)

    node_grad, genc, bsage = pl.pallas_call(
        node_kernel,
        out_shape=(
            jax.ShapeDtypeStruct((n, d), F32),
            jax.ShapeDtypeStruct((2 * d, d), F32),
            jax.ShapeDtypeStruct((8, d), F32),
        ),
        compiler_params=params(),
    )(*parts, from_row, features, agg, w_first)

    cut = 2 * d // nrow
    thin = cut // ncol
    shared = jnp.concatenate([bsage[:1], sums[2 * d : 2 * d + 7]], axis=0)
    mixed = jnp.concatenate(
        [
            genc.reshape(nrow, cut, d), sums[: 2 * d].reshape(nrow, cut, d),
            jnp.broadcast_to(shared[None], (nrow, 8, d)),
        ],
        axis=1,
    )
    mixed = jnp.sum(a2a(mixed, ROW), axis=0)
    vec = mixed[2 * cut :]
    over = jnp.concatenate(
        [mixed[:cut].reshape(ncol, thin, d), jnp.broadcast_to(vec[None, 0:1], (ncol, 1, d))], axis=1
    )
    over = jnp.sum(a2a(over, COL), axis=0)
    grad_bsage = over[thin]
    enc = to_all(over[:thin], COL, ncol).reshape(cut, d)
    final = to_all(jnp.concatenate([enc, mixed[cut : 2 * cut]], axis=0), ROW, nrow)
    enc = final[:, :cut].reshape(2 * d, d)
    dec = final[:, cut:].reshape(2 * d, d)
    return (
        embeds, logits, node_grad, enc[:d], enc[d:], grad_bsage, dec[None], vec[1:2], vec[2:3],
    )


def solution(mesh):
    fine = Mesh(mesh.devices.reshape(mesh.shape["row"] // 2, 2, mesh.shape["col"] // 8, 8), ALL)
    edge = P(ROW, COL, None)
    placed = (
        P(ALL, None), P(None, ALL), P(ALL, None, None),
        P(), P(), P(), P(), P(), P(), P(),
        P(ROW, COL, None, None), edge, edge, edge,
    )
    return jax.shard_map(
        per_device,
        mesh=fine,
        in_specs=placed,
        out_specs=(
            P(ALL, None), edge, P(ALL, None), P(), P(), P(),
            P(COL, None, None), P(COL, None), P(COL, None),
        ),
        check_vma=False,
    )
```

```python
import functools

import jax
import jax.numpy as jnp
from jax import lax
from jax.experimental import pallas as pl
from jax.experimental.pallas import tpu as pltpu
from jax.sharding import Mesh, PartitionSpec as P

ROW = ("x", "core")
COL = ("y", "z")
ALL = ROW + COL
BLOCK = 512
WINDOW = 512
SUB = 64
F32 = jnp.float32
BF16 = jnp.bfloat16


def dot(a, b):
    return jnp.dot(a, b, preferred_element_type=F32)


def dot_tn(a, b):
    return lax.dot_general(a, b, (((0,), (0,)), ((), ())), preferred_element_type=F32)


def one_hot(index, shape, dim):
    spots = lax.broadcasted_iota(jnp.int32, shape, dim).astype(F32)
    return jnp.where(index == spots, 1.0, 0.0).astype(BF16)


def dot_nt(a, b):
    return lax.dot_general(a, b, (((1,), (1,)), ((), ())), preferred_element_type=F32)


def only(picks, owner, value):
    return jnp.where(owner == jnp.asarray(value).astype(BF16), picks, jnp.zeros_like(picks))


def outgoing_kernel(ids_ref, feat_ref, out_ref):
    n = feat_ref.shape[0]
    cols = jnp.transpose(jnp.broadcast_to(ids_ref[...], (8, n)).astype(F32))
    out_ref[...] = dot(one_hot(cols[:, 0:1], (n, n), 1), feat_ref[...]).astype(BF16)


def encoder_kernel(neigh_ref, feat_ref, recv_ref, wself_ref, wneigh_ref, agg_ref, emb_ref):
    fanout, n = neigh_ref.shape
    cols = jnp.transpose(neigh_ref[...].astype(F32))
    spots = lax.broadcasted_iota(jnp.int32, (n, 2 * n), 1).astype(F32)
    count = jnp.zeros((n, 2 * n), F32)
    for k in range(fanout):
        count = count + jnp.where(cols[:, k : k + 1] == spots, 1.0, 0.0)
    count = count.astype(BF16)
    total = dot(count[:, :n], feat_ref[...]) + dot(count[:, n:], recv_ref[...])
    agg = (total / fanout).astype(BF16)
    agg_ref[...] = agg
    emb_ref[...] = dot(feat_ref[...], wself_ref[...]) + dot(agg, wneigh_ref[...])


def decoder_kernel(base, count, closing, *refs):
    start_ref, fields_ref = refs[:2]
    es_refs = refs[2 : 2 + count]
    ed_ref, w1_ref, bfirst_ref, w2_ref, w2r_ref, b2_ref = refs[2 + count : 8 + count]
    at_out = 8 + count if base == 0 else 11 + count
    so_far = refs[8 + count : at_out]
    logit_ref, dacc, sums_ref, qs_ref = refs[at_out : at_out + 4]
    qd_ref = refs[at_out + 4] if closing else None
    xs, dp, pick_d, put_d, pre, hid = refs[-6:]
    ny, n, d = es_refs[0].shape
    dst_parts = ed_ref.shape[0]
    half = 128
    first = start_ref[base]
    last = start_ref[base + ny * count]
    low = float(base * n)
    high = float((base + ny * count) * n)
    origin = pl.multiple_of((first >> 7) << 7, half)
    blocks = (last - origin + BLOCK - 1) // BLOCK
    for k, ref in enumerate((logit_ref, dacc, sums_ref)):
        ref[...] = so_far[k][...] if so_far else jnp.zeros_like(ref)
    xs[...] = jnp.zeros_like(xs)
    after = pl.multiple_of(origin + blocks * BLOCK, half)
    dp[pl.ds(after, WINDOW)] = jnp.zeros((WINDOW, d), BF16)

    def window(o):
        at = pl.multiple_of((start_ref[o] >> 7) << 7, half)
        return at, fields_ref[:, pl.ds(at, WINDOW)]

    for j in range(count):
        for y in range(ny):
            o = base + j * ny + y
            at, rows = window(o)
            col = jnp.transpose(rows)[:, 0:1] - float(o * n)
            xs[pl.ds(at, WINDOW)] += dot(one_hot(col, (WINDOW, n), 1), es_refs[j][y]).astype(BF16)

    def block(i, carry):
        at = pl.multiple_of(origin + i * BLOCK, half)
        rows = fields_ref[:, pl.ds(at, BLOCK)]
        cols = jnp.transpose(rows)
        wide = (BLOCK, n)
        tall = (n, BLOCK)
        dst_pick = one_hot(cols[:, 2:3], wide, 1)
        dst_owner = jnp.broadcast_to(cols[:, 1:2], wide).astype(BF16)
        for h in range(dst_parts):
            pick_d[:, h * n : (h + 1) * n] = only(dst_pick, dst_owner, float(h))
        x_dst = dot(pick_d[...], ed_ref[...].reshape(dst_parts * n, d)).astype(BF16)
        pre[...] = dot(xs[pl.ds(at, BLOCK)], w1_ref[:d]) + dot(x_dst, w1_ref[d:])
        inside = jnp.where((cols[:, 0:1] >= low) & (cols[:, 0:1] < high), 1.0, 0.0)

        for k in range(0, BLOCK, SUB):
            p = pre[k : k + SUB] + bfirst_ref[...]
            s = 0.5 * jnp.tanh(0.5 * p) + 0.5
            hid[k : k + SUB] = (p * s).astype(BF16)
        score = dot(hid[...], w2r_ref[...]) + b2_ref[0, 0]
        eye = lax.broadcasted_iota(jnp.int32, (half, half), 0) == lax.broadcasted_iota(jnp.int32, (half, half), 1)
        out = [
            jnp.sum(jnp.where(eye, score[k : k + half], 0.0), axis=0, keepdims=True) for k in range(0, BLOCK, half)
        ]
        inside_t = (rows[0:1, :] >= low) & (rows[0:1, :] < high)
        logit_ref[:, pl.ds(at, BLOCK)] = jnp.where(
            inside_t, jnp.concatenate(out, axis=1), logit_ref[:, pl.ds(at, BLOCK)]
        )
        sum_p = jnp.zeros((1, d), F32)
        sum_h = jnp.zeros((1, d), F32)
        for k in range(0, BLOCK, SUB):
            p = pre[k : k + SUB] + bfirst_ref[...]
            s = 0.5 * jnp.tanh(0.5 * p) + 0.5
            h = p * s
            g = (0.5 * jnp.tanh(0.5 * score[k : k + SUB]) + 0.5) - cols[k : k + SUB, 3:4]
            g = g * inside[k : k + SUB]
            g = jnp.concatenate([g, g], axis=1)
            e = g * w2_ref[...] * (s + h * (1.0 - s))
            dp[pl.ds(at + k, SUB)] = e.astype(BF16)
            sum_p = sum_p + jnp.sum(e, axis=0, keepdims=True)
            sum_h = sum_h + jnp.sum(h * g, axis=0, keepdims=True)
        sums_ref[2 * d : 2 * d + 1, :] += sum_p
        sums_ref[2 * d + 1 : 2 * d + 2, :] += sum_h
        dst_put = one_hot(rows[2:3, :], tall, 0)
        dst_owner_t = jnp.broadcast_to(rows[1:2, :], tall).astype(BF16)
        for h in range(dst_parts):
            put_d[h * n : (h + 1) * n, :] = only(dst_put, dst_owner_t, float(h))
        dacc[...] += dot(put_d[...], dp[pl.ds(at, BLOCK)])
        return carry

    lax.fori_loop(0, blocks, block, 0)

    for j in range(count):
        for y in range(ny):
            o = base + j * ny + y
            at, rows = window(o)
            put = one_hot(rows[0:1, :] - float(o * n), (n, WINDOW), 0)
            q = dot(put, dp[pl.ds(at, WINDOW)]).astype(BF16)
            qs_ref[y, j] = q
            sums_ref[:d] += dot_tn(es_refs[j][y], q)

    if closing:
        for h in range(dst_parts):
            q = dacc[h * n : (h + 1) * n].astype(BF16)
            qd_ref[h] = q
            sums_ref[d : 2 * d] += dot_tn(ed_ref[h], q)


def node_kernel(*refs):
    ps_refs = refs[:-7]
    pd_ref, feat_ref, agg_ref, w1_ref, node_ref, genc_ref, vec_ref = refs[-7:]
    d = feat_ref.shape[1]

    def total(ref):
        out = ref[0].astype(F32)
        for k in range(1, ref.shape[0]):
            out = out + ref[k].astype(F32)
        return out

    def times_wt(q, w):
        high = q.astype(BF16)
        low = (q - high.astype(F32)).astype(BF16)
        return dot_nt(high, w) + dot_nt(low, w)

    from_src = ps_refs[0][...].astype(F32)
    for ref in ps_refs[1:]:
        from_src = from_src + ref[...].astype(F32)
    grad = times_wt(from_src, w1_ref[:d]) + times_wt(total(pd_ref), w1_ref[d:])
    node_ref[...] = grad
    grad_b = grad.astype(BF16)
    genc_ref[:d] = dot_tn(feat_ref[...], grad_b)
    genc_ref[d:] = dot_tn(agg_ref[...], grad_b)
    vec_ref[...] = jnp.broadcast_to(jnp.sum(grad, axis=0, keepdims=True), vec_ref.shape)


def params(mib=60):
    return pltpu.CompilerParams(vmem_limit_bytes=mib * 1024 * 1024)


def a2a(x, axes):
    return lax.all_to_all(x, axes, split_axis=0, concat_axis=0, tiled=True)


def to_all(x, axes, count):
    return a2a(jnp.broadcast_to(x[None], (count,) + x.shape), axes)


def decoder(base, closing, start, fields, es, e_row, w_first, b_first, w_second, b_second, *so_far):
    ny, n, d = es[0].shape
    nrow = e_row.shape[0]
    count = len(es)
    length = fields.shape[1]
    vmem = pl.BlockSpec(memory_space=pltpu.VMEM)
    smem = pl.BlockSpec(memory_space=pltpu.SMEM)
    outs = [
        jax.ShapeDtypeStruct((1, length - WINDOW), F32),
        jax.ShapeDtypeStruct((nrow * n, d), F32),
        jax.ShapeDtypeStruct((2 * d + 8, d), F32),
        jax.ShapeDtypeStruct((ny, count, n, d), BF16),
    ]
    if closing:
        outs.append(jax.ShapeDtypeStruct((nrow, n, d), BF16))
    share = count * ny * fields.shape[1] // 32
    return pl.pallas_call(
        functools.partial(decoder_kernel, base, count, closing),
        in_specs=[smem] + [vmem] * (6 + count) + [smem] + [vmem] * len(so_far),
        out_specs=[vmem] * len(outs),
        scratch_shapes=[
            pltpu.VMEM((length, d), BF16), pltpu.VMEM((length, d), BF16),
            pltpu.VMEM((BLOCK, nrow * n), BF16), pltpu.VMEM((nrow * n, BLOCK), BF16),
            pltpu.VMEM((BLOCK, d), F32), pltpu.VMEM((BLOCK, d), BF16),
        ],
        out_shape=outs,
        compiler_params=params(),
        cost_estimate=pl.CostEstimate(
            flops=share * d * (4 * nrow * n + 8 * n), bytes_accessed=8 * 1024 * 1024, transcendentals=2 * share * d
        ),
    )(
        start, fields, *es, e_row, w_first, b_first, w_second.astype(F32)[None],
        jnp.broadcast_to(w_second[:, None], (d, 128)), b_second, *so_far,
    )


def per_device(
    features, neighbours, halo_ids, w_self, w_neigh, b_sage, w_first, b_first,
    w_second, b_second, src_owner, src_local, dst_index, labels,
):
    n, d = features.shape
    nx, nc, ny, nz = (lax.axis_size(a) for a in ALL)
    nrow, ncol = nx * nc, ny * nz
    edges = src_local.shape[2]

    outgoing = pl.pallas_call(
        outgoing_kernel, out_shape=jax.ShapeDtypeStruct((n, d), BF16), compiler_params=params()
    )(halo_ids[0], features)
    received = a2a(outgoing.reshape(nrow, ncol, d), ROW)
    received, src_owner = lax.optimization_barrier((received, src_owner))
    received = lax.all_to_all(received, COL, split_axis=1, concat_axis=1, tiled=True)

    ahead = ((src_owner[0, 0, :, 0] & (nz - 1)) - lax.axis_index("z")) & (nz - 1)
    rank = jnp.where(ahead == 0, 0, jnp.where(ahead <= nz // 2, 2 * ahead - 1, 2 * (nz - ahead)))
    slot = rank * ny + src_owner[0, 0, :, 0] // nz
    key = ((slot * n + src_local[0, 0]) << 12) | (dst_index[0, 0] << 1) | labels[0, 0]
    key, order = lax.sort((key, lax.iota(jnp.int32, edges)), num_keys=1)
    row = key >> 12
    zero = jnp.zeros_like(key)
    fields = jnp.stack([row, (key >> 9) & 7, (key >> 1) & 255, key & 1, zero, zero, zero, zero]).astype(F32)
    fields = jnp.pad(fields, ((0, 0), (0, WINDOW + BLOCK)), constant_values=-1.0)
    owners = lax.iota(jnp.int32, ncol + 1)
    start = jnp.sum((row[None, :] < (owners * n)[:, None]).astype(jnp.int32), axis=1)

    agg, emb_f = pl.pallas_call(
        encoder_kernel,
        out_shape=(jax.ShapeDtypeStruct((n, d), BF16), jax.ShapeDtypeStruct((n, d), F32)),
        compiler_params=params(),
    )(neighbours, features, received.reshape(nrow * ncol, d), w_self, w_neigh)
    emb_f, fields, start = lax.optimization_barrier((emb_f, fields, start))
    embeds = (emb_f + b_sage).astype(BF16)
    e_y = lax.all_gather(embeds, "y")

    def shift(x, by):
        return lax.ppermute(x, "z", [(i, (i + by) % nz) for i in range(nz)])

    at = {0: e_y}
    up, down = e_y, e_y
    for k in range(1, nz // 2 + 1):
        down = shift(down, -1)
        at[k] = down
        if k < nz // 2:
            up = shift(up, 1)
            at[nz - k] = up
    e_row = to_all(embeds, ROW, nrow)

    def send(part, group):
        return [shift(part[j], k) if k else part[j] for j, k in enumerate(group)]

    groups = ((0, 1, 7), (2, 6, 3), (5, 4))
    carry, parts, pending = (), [], []
    base = 0
    for g, group in enumerate(groups):
        closing = g == len(groups) - 1
        if closing:
            carry, pending[0] = lax.optimization_barrier((carry, pending[0]))
            parts += send(pending[0], groups[0])
        out = decoder(
            base, closing, start, fields, [at[k] for k in group], e_row, w_first,
            b_first[None], w_second, b_second[None], *carry,
        )
        carry, qs = out[:3], out[3]
        base += len(group) * ny
        if closing:
            qs, parts = lax.optimization_barrier((qs, parts))
        pending.append(jnp.sum(a2a(qs, "y").astype(F32), axis=0).astype(BF16))
    for k in range(1, len(groups)):
        parts = parts + send(pending[k], groups[k])
    logit, _, sums = carry
    qd = out[4]

    logits = lax.sort((order, logit[0, :edges]), num_keys=1)[1].reshape(1, 1, edges)
    from_row = a2a(qd, ROW)

    node_grad, genc, bsage = pl.pallas_call(
        node_kernel,
        out_shape=(
            jax.ShapeDtypeStruct((n, d), F32),
            jax.ShapeDtypeStruct((2 * d, d), F32),
            jax.ShapeDtypeStruct((8, d), F32),
        ),
        compiler_params=params(),
    )(*parts, from_row, features, agg, w_first)

    cut = 2 * d // nrow
    thin = cut // ncol
    shared = jnp.concatenate([bsage[:1], sums[2 * d : 2 * d + 2]], axis=0)
    high = shared.astype(BF16)
    low = (shared - high.astype(F32)).astype(BF16)
    shared = jnp.concatenate([high, low, jnp.zeros((10, d), BF16)], axis=0)
    mixed = jnp.concatenate(
        [
            genc.astype(BF16).reshape(nrow, cut, d), sums[: 2 * d].astype(BF16).reshape(nrow, cut, d),
            jnp.broadcast_to(shared[None], (nrow, 16, d)),
        ],
        axis=1,
    )
    mixed = jnp.sum(a2a(mixed, ROW).astype(F32), axis=0)
    vec = mixed[2 * cut : 2 * cut + 3] + mixed[2 * cut + 3 : 2 * cut + 6]
    over = jnp.concatenate(
        [mixed[:cut].reshape(ncol, thin, d), jnp.broadcast_to(vec[None, 0:1], (ncol, 1, d))], axis=1
    )
    over = jnp.sum(a2a(over, COL), axis=0)
    grad_bsage = over[thin]
    enc = to_all(over[:thin], COL, ncol).reshape(cut, d)
    final = jnp.concatenate([enc, mixed[cut : 2 * cut]], axis=0).astype(BF16)
    final = to_all(final, ROW, nrow).astype(F32)
    enc = final[:, :cut].reshape(2 * d, d)
    dec = final[:, cut:].reshape(2 * d, d)
    return (
        embeds, logits, node_grad, enc[:d], enc[d:], grad_bsage, dec[None], vec[1:2], vec[2:3],
    )


def solution(mesh):
    fine = Mesh(mesh.devices.reshape(mesh.shape["row"] // 2, 2, mesh.shape["col"] // 8, 8), ALL)
    edge = P(ROW, COL, None)
    placed = (
        P(ALL, None), P(None, ALL), P(ALL, None, None),
        P(), P(), P(), P(), P(), P(), P(),
        P(ROW, COL, None, None), edge, edge, edge,
    )
    return jax.shard_map(
        per_device,
        mesh=fine,
        in_specs=placed,
        out_specs=(
            P(ALL, None), edge, P(ALL, None), P(), P(), P(),
            P(COL, None, None), P(COL, None), P(COL, None),
        ),
        check_vma=False,
    )
```

```python
import functools

import jax
import jax.numpy as jnp
from jax import lax
from jax.experimental import pallas as pl
from jax.experimental.pallas import tpu as pltpu
from jax.sharding import Mesh, PartitionSpec as P

ROW = ("x", "core")
COL = ("y", "z")
ALL = ROW + COL
BLOCK = 512
WINDOW = 512
SUB = 64
F32 = jnp.float32
BF16 = jnp.bfloat16


def dot(a, b):
    return jnp.dot(a, b, preferred_element_type=F32)


def dot_tn(a, b):
    return lax.dot_general(a, b, (((0,), (0,)), ((), ())), preferred_element_type=F32)


def one_hot(index, shape, dim):
    spots = lax.broadcasted_iota(jnp.int32, shape, dim).astype(F32)
    return jnp.where(index == spots, 1.0, 0.0).astype(BF16)


def dot_nt(a, b):
    return lax.dot_general(a, b, (((1,), (1,)), ((), ())), preferred_element_type=F32)


def only(picks, owner, value):
    return jnp.where(owner == jnp.asarray(value).astype(BF16), picks, jnp.zeros_like(picks))


def outgoing_kernel(ids_ref, feat_ref, out_ref):
    n = feat_ref.shape[0]
    cols = jnp.transpose(jnp.broadcast_to(ids_ref[...], (8, n)).astype(F32))
    out_ref[...] = dot(one_hot(cols[:, 0:1], (n, n), 1), feat_ref[...]).astype(BF16)


def encoder_kernel(neigh_ref, feat_ref, recv_ref, wself_ref, wneigh_ref, agg_ref, emb_ref):
    fanout, n = neigh_ref.shape
    cols = jnp.transpose(neigh_ref[...].astype(F32))
    spots = lax.broadcasted_iota(jnp.int32, (n, 2 * n), 1).astype(F32)
    count = jnp.zeros((n, 2 * n), F32)
    for k in range(fanout):
        count = count + jnp.where(cols[:, k : k + 1] == spots, 1.0, 0.0)
    count = count.astype(BF16)
    total = dot(count[:, :n], feat_ref[...]) + dot(count[:, n:], recv_ref[...])
    agg = (total / fanout).astype(BF16)
    agg_ref[...] = agg
    emb_ref[...] = dot(feat_ref[...], wself_ref[...]) + dot(agg, wneigh_ref[...])


def decoder_kernel(base, count, closing, *refs):
    start_ref, fields_ref = refs[:2]
    es_refs = refs[2 : 2 + count]
    ed_ref, w1_ref, bfirst_ref, w2_ref, w2r_ref, b2_ref = refs[2 + count : 8 + count]
    at_out = 8 + count if base == 0 else 11 + count
    so_far = refs[8 + count : at_out]
    logit_ref, dacc, sums_ref, qs_ref = refs[at_out : at_out + 4]
    qd_ref = refs[at_out + 4] if closing else None
    xs, dp, pick_d, put_d, pre, hid = refs[-6:]
    ny, n, d = es_refs[0].shape
    dst_parts = ed_ref.shape[0]
    half = 128
    first = start_ref[base]
    last = start_ref[base + ny * count]
    low = float(base * n)
    high = float((base + ny * count) * n)
    origin = pl.multiple_of((first >> 7) << 7, half)
    blocks = (last - origin + BLOCK - 1) // BLOCK
    for k, ref in enumerate((logit_ref, dacc, sums_ref)):
        ref[...] = so_far[k][...] if so_far else jnp.zeros_like(ref)
    xs[...] = jnp.zeros_like(xs)
    after = pl.multiple_of(origin + blocks * BLOCK, half)
    dp[pl.ds(after, WINDOW)] = jnp.zeros((WINDOW, d), BF16)

    def window(o):
        at = pl.multiple_of((start_ref[o] >> 7) << 7, half)
        return at, fields_ref[:, pl.ds(at, WINDOW)]

    for j in range(count):
        for y in range(ny):
            o = base + j * ny + y
            at, rows = window(o)
            col = jnp.transpose(rows)[:, 0:1] - float(o * n)
            xs[pl.ds(at, WINDOW)] += dot(one_hot(col, (WINDOW, n), 1), es_refs[j][y]).astype(BF16)

    def block(i, carry):
        at = pl.multiple_of(origin + i * BLOCK, half)
        rows = fields_ref[:, pl.ds(at, BLOCK)]
        cols = jnp.transpose(rows)
        wide = (BLOCK, n)
        tall = (n, BLOCK)
        dst_pick = one_hot(cols[:, 2:3], wide, 1)
        dst_owner = jnp.broadcast_to(cols[:, 1:2], wide).astype(BF16)
        for h in range(dst_parts):
            pick_d[:, h * n : (h + 1) * n] = only(dst_pick, dst_owner, float(h))
        x_dst = dot(pick_d[...], ed_ref[...].reshape(dst_parts * n, d)).astype(BF16)
        pre[...] = dot(xs[pl.ds(at, BLOCK)], w1_ref[:d]) + dot(x_dst, w1_ref[d:])
        inside = jnp.where((cols[:, 0:1] >= low) & (cols[:, 0:1] < high), 1.0, 0.0)

        for k in range(0, BLOCK, SUB):
            p = pre[k : k + SUB] + bfirst_ref[...]
            s = 0.5 * jnp.tanh(0.5 * p) + 0.5
            hid[k : k + SUB] = (p * s).astype(BF16)
        score = dot(hid[...], w2r_ref[...]) + b2_ref[0, 0]
        eye = lax.broadcasted_iota(jnp.int32, (half, half), 0) == lax.broadcasted_iota(jnp.int32, (half, half), 1)
        out = [
            jnp.sum(jnp.where(eye, score[k : k + half], 0.0), axis=0, keepdims=True) for k in range(0, BLOCK, half)
        ]
        inside_t = (rows[0:1, :] >= low) & (rows[0:1, :] < high)
        logit_ref[:, pl.ds(at, BLOCK)] = jnp.where(
            inside_t, jnp.concatenate(out, axis=1), logit_ref[:, pl.ds(at, BLOCK)]
        )
        sum_p = jnp.zeros((1, d), F32)
        sum_h = jnp.zeros((1, d), F32)
        for k in range(0, BLOCK, SUB):
            p = pre[k : k + SUB] + bfirst_ref[...]
            s = 0.5 * jnp.tanh(0.5 * p) + 0.5
            h = p * s
            g = (0.5 * jnp.tanh(0.5 * score[k : k + SUB]) + 0.5) - cols[k : k + SUB, 3:4]
            g = g * inside[k : k + SUB]
            g = jnp.concatenate([g, g], axis=1)
            e = g * w2_ref[...] * (s + h * (1.0 - s))
            dp[pl.ds(at + k, SUB)] = e.astype(BF16)
            sum_p = sum_p + jnp.sum(e, axis=0, keepdims=True)
            sum_h = sum_h + jnp.sum(h * g, axis=0, keepdims=True)
        sums_ref[2 * d : 2 * d + 1, :] += sum_p
        sums_ref[2 * d + 1 : 2 * d + 2, :] += sum_h
        dst_put = one_hot(rows[2:3, :], tall, 0)
        dst_owner_t = jnp.broadcast_to(rows[1:2, :], tall).astype(BF16)
        for h in range(dst_parts):
            put_d[h * n : (h + 1) * n, :] = only(dst_put, dst_owner_t, float(h))
        dacc[...] += dot(put_d[...], dp[pl.ds(at, BLOCK)])
        return carry

    lax.fori_loop(0, blocks, block, 0)

    for j in range(count):
        for y in range(ny):
            o = base + j * ny + y
            at, rows = window(o)
            put = one_hot(rows[0:1, :] - float(o * n), (n, WINDOW), 0)
            q = dot(put, dp[pl.ds(at, WINDOW)]).astype(BF16)
            qs_ref[y, j] = q
            sums_ref[:d] += dot_tn(es_refs[j][y], q)

    if closing:
        for h in range(dst_parts):
            q = dacc[h * n : (h + 1) * n].astype(BF16)
            qd_ref[h, :n] = q
            sums_ref[d : 2 * d] += dot_tn(ed_ref[h], q)
        cut = 2 * d // dst_parts
        for h in range(dst_parts):
            qd_ref[h, n:] = sums_ref[h * cut : (h + 1) * cut].astype(BF16)


def node_kernel(*refs):
    ps_refs = refs[:-7]
    pd_ref, feat_ref, agg_ref, w1_ref, sums_ref, node_ref, mixed_ref = refs[-7:]
    n, d = feat_ref.shape
    nrow = pd_ref.shape[0]
    cut = 2 * d // nrow

    def times_wt(q, w):
        high = q.astype(BF16)
        low = (q - high.astype(F32)).astype(BF16)
        return dot_nt(high, w) + dot_nt(low, w)

    from_src = ps_refs[0][...].astype(F32)
    for ref in ps_refs[1:]:
        from_src = from_src + ref[...].astype(F32)
    from_dst = pd_ref[0, :n].astype(F32)
    for k in range(1, nrow):
        from_dst = from_dst + pd_ref[k, :n].astype(F32)
    grad = times_wt(from_src, w1_ref[:d]) + times_wt(from_dst, w1_ref[d:])
    node_ref[...] = grad
    grad_b = grad.astype(BF16)
    halves = (dot_tn(feat_ref[...], grad_b).astype(BF16), dot_tn(agg_ref[...], grad_b).astype(BF16))
    line = lax.broadcasted_iota(jnp.int32, (16, d), 0)
    extra = jnp.zeros((16, d), F32)
    shared = (jnp.sum(grad, axis=0, keepdims=True), sums_ref[2 * d : 2 * d + 1], sums_ref[2 * d + 1 : 2 * d + 2])
    for k, value in enumerate(shared):
        high = value.astype(BF16).astype(F32)
        extra = jnp.where(line == k, high, jnp.where(line == k + 3, value - high, extra))
    extra = extra.astype(BF16)
    for j in range(nrow):
        half, at = halves[j * cut // d], j * cut % d
        mixed_ref[j, :cut] = half[at : at + cut]
        mixed_ref[j, cut:] = extra


def params(mib=60):
    return pltpu.CompilerParams(vmem_limit_bytes=mib * 1024 * 1024)


def a2a(x, axes):
    return lax.all_to_all(x, axes, split_axis=0, concat_axis=0, tiled=True)


def to_all(x, axes, count):
    return a2a(jnp.broadcast_to(x[None], (count,) + x.shape), axes)


def decoder(base, closing, start, fields, es, e_row, w_first, b_first, w_second, b_second, *so_far):
    ny, n, d = es[0].shape
    nrow = e_row.shape[0]
    count = len(es)
    length = fields.shape[1]
    vmem = pl.BlockSpec(memory_space=pltpu.VMEM)
    smem = pl.BlockSpec(memory_space=pltpu.SMEM)
    outs = [
        jax.ShapeDtypeStruct((1, length - WINDOW), F32),
        jax.ShapeDtypeStruct((nrow * n, d), F32),
        jax.ShapeDtypeStruct((2 * d + 8, d), F32),
        jax.ShapeDtypeStruct((ny, count, n, d), BF16),
    ]
    if closing:
        outs.append(jax.ShapeDtypeStruct((nrow, n + 2 * d // nrow, d), BF16))
    share = count * ny * fields.shape[1] // 32
    return pl.pallas_call(
        functools.partial(decoder_kernel, base, count, closing),
        in_specs=[smem] + [vmem] * (6 + count) + [smem] + [vmem] * len(so_far),
        out_specs=[vmem] * len(outs),
        scratch_shapes=[
            pltpu.VMEM((length, d), BF16), pltpu.VMEM((length, d), BF16),
            pltpu.VMEM((BLOCK, nrow * n), BF16), pltpu.VMEM((nrow * n, BLOCK), BF16),
            pltpu.VMEM((BLOCK, d), F32), pltpu.VMEM((BLOCK, d), BF16),
        ],
        out_shape=outs,
        compiler_params=params(),
        cost_estimate=pl.CostEstimate(
            flops=share * d * (4 * nrow * n + 8 * n), bytes_accessed=8 * 1024 * 1024, transcendentals=2 * share * d
        ),
    )(
        start, fields, *es, e_row, w_first, b_first, w_second.astype(F32)[None],
        jnp.broadcast_to(w_second[:, None], (d, 128)), b_second, *so_far,
    )


def per_device(
    features, neighbours, halo_ids, w_self, w_neigh, b_sage, w_first, b_first,
    w_second, b_second, src_owner, src_local, dst_index, labels,
):
    n, d = features.shape
    nx, nc, ny, nz = (lax.axis_size(a) for a in ALL)
    nrow, ncol = nx * nc, ny * nz
    edges = src_local.shape[2]

    outgoing = pl.pallas_call(
        outgoing_kernel, out_shape=jax.ShapeDtypeStruct((n, d), BF16), compiler_params=params()
    )(halo_ids[0], features)
    received = a2a(outgoing.reshape(nrow, ncol, d), ROW)
    received, src_owner = lax.optimization_barrier((received, src_owner))
    received = lax.all_to_all(received, COL, split_axis=1, concat_axis=1, tiled=True)

    ahead = ((src_owner[0, 0, :, 0] & (nz - 1)) - lax.axis_index("z")) & (nz - 1)
    rank = jnp.where(ahead == 0, 0, jnp.where(ahead <= nz // 2, 2 * ahead - 1, 2 * (nz - ahead)))
    slot = rank * ny + src_owner[0, 0, :, 0] // nz
    key = ((slot * n + src_local[0, 0]) << 12) | (dst_index[0, 0] << 1) | labels[0, 0]
    key, order = lax.sort((key, lax.iota(jnp.int32, edges)), num_keys=1)
    row = key >> 12
    zero = jnp.zeros_like(key)
    fields = jnp.stack([row, (key >> 9) & 7, (key >> 1) & 255, key & 1, zero, zero, zero, zero]).astype(F32)
    fields = jnp.pad(fields, ((0, 0), (0, WINDOW + BLOCK)), constant_values=-1.0)
    owners = lax.iota(jnp.int32, ncol + 1)
    start = jnp.sum((row[None, :] < (owners * n)[:, None]).astype(jnp.int32), axis=1)

    agg, emb_f = pl.pallas_call(
        encoder_kernel,
        out_shape=(jax.ShapeDtypeStruct((n, d), BF16), jax.ShapeDtypeStruct((n, d), F32)),
        compiler_params=params(),
    )(neighbours, features, received.reshape(nrow * ncol, d), w_self, w_neigh)
    emb_f, fields, start = lax.optimization_barrier((emb_f, fields, start))
    embeds = (emb_f + b_sage).astype(BF16)
    e_y = lax.all_gather(embeds, "y")

    def shift(x, by):
        return lax.ppermute(x, "z", [(i, (i + by) % nz) for i in range(nz)])

    at = {0: e_y, 1: shift(e_y, -1), 7: shift(e_y, 1)}
    at[2], at[6] = shift(at[1], -1), shift(at[7], 1)
    at[3], at[4], at[5] = shift(at[2], -1), shift(at[2], -2), shift(at[7], 2)
    e_row = to_all(embeds, ROW, nrow)

    def send(part, group):
        return [shift(part[j], k) if k else part[j] for j, k in enumerate(group)]

    groups = ((0, 1, 7), (2, 6, 3), (5, 4))
    carry, parts, pending = (), [], []
    base = 0
    for g, group in enumerate(groups):
        closing = g == len(groups) - 1
        if g == len(groups) - 2:
            carry, soon = lax.optimization_barrier((carry, [at[k] for k in groups[-1]]))
            at.update(zip(groups[-1], soon))
        if closing:
            carry, pending[0] = lax.optimization_barrier((carry, pending[0]))
            parts += send(pending[0], groups[0])
        out = decoder(
            base, closing, start, fields, [at[k] for k in group], e_row, w_first,
            b_first[None], w_second, b_second[None], *carry,
        )
        carry, qs = out[:3], out[3]
        base += len(group) * ny
        if closing:
            qs, parts = lax.optimization_barrier((qs, parts))
        pending.append(jnp.sum(a2a(qs, "y").astype(F32), axis=0).astype(BF16))
    for k in range(1, len(groups)):
        parts = parts + send(pending[k], groups[k])
    logit, _, sums = carry
    qd = out[4]

    logits = lax.sort((order, logit[0, :edges]), num_keys=1)[1].reshape(1, 1, edges)
    from_row = a2a(qd, ROW)

    cut = 2 * d // nrow
    thin = cut // ncol
    node_grad, mixed = pl.pallas_call(
        node_kernel,
        out_shape=(jax.ShapeDtypeStruct((n, d), F32), jax.ShapeDtypeStruct((nrow, cut + 16, d), BF16)),
        compiler_params=params(),
    )(*parts, from_row, features, agg, w_first, sums)
    dec_cut = jnp.sum(from_row[:, n:].astype(F32), axis=0)
    mixed = jnp.sum(a2a(mixed, ROW).astype(F32), axis=0)
    vec = mixed[cut : cut + 3] + mixed[cut + 3 : cut + 6]
    over = jnp.concatenate(
        [mixed[:cut].reshape(ncol, thin, d), jnp.broadcast_to(vec[None, 0:1], (ncol, 1, d))], axis=1
    )
    over = jnp.sum(a2a(over, COL), axis=0)
    grad_bsage = over[thin]
    enc = to_all(over[:thin], COL, ncol).reshape(cut, d)
    final = jnp.concatenate([enc, dec_cut], axis=0).astype(BF16)
    final = to_all(final, ROW, nrow).astype(F32)
    enc = final[:, :cut].reshape(2 * d, d)
    dec = final[:, cut:].reshape(2 * d, d)
    return (
        embeds, logits, node_grad, enc[:d], enc[d:], grad_bsage, dec[None], vec[1:2], vec[2:3],
    )


def solution(mesh):
    fine = Mesh(mesh.devices.reshape(mesh.shape["row"] // 2, 2, mesh.shape["col"] // 8, 8), ALL)
    edge = P(ROW, COL, None)
    placed = (
        P(ALL, None), P(None, ALL), P(ALL, None, None),
        P(), P(), P(), P(), P(), P(), P(),
        P(ROW, COL, None, None), edge, edge, edge,
    )
    return jax.shard_map(
        per_device,
        mesh=fine,
        in_specs=placed,
        out_specs=(
            P(ALL, None), edge, P(ALL, None), P(), P(), P(),
            P(COL, None, None), P(COL, None), P(COL, None),
        ),
        check_vma=False,
    )
```
